32 devices in a mesh: dp: 8 (over y, x, core), fsdp: 4 (over z).
Axes of the slice: x: 2, y: 2, z: 4, core: 2. Of those that a mesh axis runs over, the one named last changes fastest.
Arguments:
- rollout_rows: bfloat16 [4096, 8192], P(('dp', 'fsdp')), may hold values from -6 to 6
- lengths: int32 [32, 8], P(('dp', 'fsdp')), may hold values from 1 to 32, as said below
- dest: int32 [32, 8], P(('dp', 'fsdp')), may hold values from 0 to 7, as said below
- offset: int32 [32, 8], P(('dp', 'fsdp')), may hold values from 0 to 96, as said below
- query: bfloat16 [4096, 4096], P(('dp', 'fsdp')), may hold values from -100 to 100
- key_rows: bfloat16 [4096, 512], P(('dp', 'fsdp')), may hold values from -5 to 5
- value_weight: bfloat16 [8192, 512], P('fsdp'), may hold values from -0.0625 to 0.0625
- d_out: bfloat16 [4096, 4096], P(('dp', 'fsdp')), may hold values from -6 to 6
Outputs:
- attn_out: bfloat16 [4096, 4096], P(('dp', 'fsdp'))
- grad_query: bfloat16 [4096, 4096], P(('dp', 'fsdp'))
- grad_key: bfloat16 [4096, 512], P(('dp', 'fsdp'))
- grad_input: bfloat16 [4096, 8192], P(('dp', 'fsdp'))
- grad_weight: float32 [8192, 512], P(('dp', 'fsdp'))
The draws below stay inside these ranges and needn't reach their ends.
Inputs may be any that keep to these rules, and one draw needn't show every extreme that they name: Each rollout device's 8 lengths sum to 128. `dest`: the learner has the sender's fsdp index; the sequences of one device go to 8 different learner devices. `offset`: the sequences that a learner device receives cover its 128 rows exactly once; on every learner device the last of them is one of 32 rows.
All inputs are finite; a program needn't handle non-finite values.
Results may differ from the reference program's by a relative error of at most 0.006.
Values may be sent and summed in bfloat16 or wider, within the bound.
A program may use at most 128 MiB of HBM per device.

```python
import math
import jax
import jax.numpy as jnp
from jax import lax

D = 8192
HEAD_SIZE = 128
QUERY_HEADS = 32
KEY_VALUE_HEADS = 4
TOK_DEV = 128
SEQ_DEV = 8
MAXLEN = 32
QW = 4096
KVW = 512
SHARDS = 32
TOKEN_ROWS = 4096
N_DP = 8
N_FSDP = 4


def order_with_longest_last(key):
    rest = jax.random.permutation(key, SEQ_DEV - 1).astype(jnp.int32) + 1
    return jnp.concatenate([rest, jnp.zeros((1,), jnp.int32)])


def balance_tables(key):
    keys = jax.random.split(jax.random.fold_in(key, 17), 4)
    remain = TOK_DEV - MAXLEN
    parts_count = SEQ_DEV - 1
    weights = jax.random.randint(keys[0], (N_FSDP, parts_count), 2, 5)
    shares = weights * remain // jnp.sum(weights, axis=1, keepdims=True)
    leftover = remain - jnp.sum(shares, axis=1, keepdims=True)
    shares = shares + (jnp.arange(parts_count)[None, :] < leftover).astype(jnp.int32)
    class_len = jnp.concatenate([jnp.full((N_FSDP, 1), MAXLEN, jnp.int32), shares.astype(jnp.int32)], axis=1)
    shifts = jax.vmap(lambda k: jax.random.permutation(k, N_DP)[:SEQ_DEV])(jax.random.split(keys[1], N_FSDP))
    orders = jax.vmap(lambda k: jax.random.permutation(k, SEQ_DEV))(jax.random.split(keys[2], SHARDS))
    learner_orders = jax.vmap(order_with_longest_last)(jax.random.split(keys[3], SHARDS))
    device_ids = jnp.arange(SHARDS)
    dp_index = device_ids // N_FSDP
    column = device_ids % N_FSDP
    own_len = class_len[column]
    seq_lengths = jnp.take_along_axis(own_len, orders, axis=1)
    targets = (dp_index[:, None] + jnp.take_along_axis(shifts[column], orders, axis=1)) % N_DP
    classes = jnp.arange(SEQ_DEV)
    positions = jnp.sum(jnp.arange(SEQ_DEV)[None, :, None] * (learner_orders[:, :, None] == classes[None, None, :]).astype(jnp.int32), axis=1)
    learner = targets * N_FSDP + column[:, None]
    learner_pos = positions[learner]
    my_pos = jnp.take_along_axis(learner_pos, orders[:, :, None], axis=2)[:, :, 0]
    earlier = (learner_pos < my_pos[:, :, None]).astype(jnp.int32)
    offsets = jnp.sum(own_len[:, None, :] * earlier, axis=2)
    return (seq_lengths.astype(jnp.int32), targets.astype(jnp.int32), offsets.astype(jnp.int32))


def draw_lengths(key, part):
    return balance_tables(key)[0]


def draw_dest(key, part):
    return balance_tables(key)[1]


def draw_offset(key, part):
    return balance_tables(key)[2]


def query_and_keys(key):
    keys = jax.random.split(jax.random.fold_in(key, 29), 2)
    sampled_keys = jax.random.truncated_normal(keys[0], -4.0, 4.0, (TOKEN_ROWS, KVW), jnp.float32)
    queries = jax.random.truncated_normal(keys[1], -4.0, 4.0, (TOKEN_ROWS, QW), jnp.float32)
    return (queries.astype(jnp.bfloat16), sampled_keys.astype(jnp.bfloat16))


def draw_query(key, part):
    return query_and_keys(key)[0]


def draw_key_rows(key, part):
    return query_and_keys(key)[1]


def block_scale(stream_key, dims, cuts, least, top_value):
    def one(dim, parts):
        heights = jax.random.uniform(jax.random.fold_in(jax.random.fold_in(stream_key, 6), dim), (parts,), jnp.float32, least / len(cuts), top_value / len(cuts))
        return jnp.repeat(jnp.exp(heights), dims[dim] // parts).reshape((-1,) + (1,) * (len(dims) - dim - 1))

    loudness = one(*cuts[0])
    for cut in cuts[1:]:
        loudness = loudness * one(*cut)
    return loudness


def bell_draw(rng, extent, spread, most, cuts=(), held_as=jnp.bfloat16):
    values = spread * jax.random.normal(rng, extent, jnp.float32)
    if cuts:
        values = values * block_scale(rng, extent, cuts, -0.22, 0.18)
    return jnp.clip(values, -most, most).astype(held_as)


def setup_inputs(seed: int = 0) -> dict:
    key_list = jax.random.split(jax.random.key(seed), 9)
    return {
        "rollout_rows": bell_draw(key_list[0], (TOKEN_ROWS, D), 1.0, 6.0, ((0, 32),)),
        "lengths": draw_lengths(jax.random.fold_in(key_list[8], 71), 0),
        "dest": draw_dest(jax.random.fold_in(key_list[8], 71), 0),
        "offset": draw_offset(jax.random.fold_in(key_list[8], 71), 0),
        "query": draw_query(jax.random.fold_in(key_list[8], 71), 0),
        "key_rows": draw_key_rows(jax.random.fold_in(key_list[8], 71), 0),
        "value_weight": bell_draw(key_list[6], (D, KVW), D ** -0.5, 0.0625, ((0, 4),)),
        "d_out": bell_draw(key_list[7], (TOKEN_ROWS, QW), 1.0, 6.0, ((0, 32),)),
    }


def attend(block_queries, block_keys, block_values, segment, gradient_block):
    row_count_total = block_queries.shape[0]
    share_ratio = QUERY_HEADS // KEY_VALUE_HEADS
    score_scale = 1.0 / math.sqrt(HEAD_SIZE)
    heads_queries = block_queries.astype(jnp.float32).reshape(row_count_total, KEY_VALUE_HEADS, share_ratio, HEAD_SIZE)
    heads_keys = block_keys.astype(jnp.float32).reshape(row_count_total, KEY_VALUE_HEADS, HEAD_SIZE)
    heads_values = block_values.astype(jnp.float32).reshape(row_count_total, KEY_VALUE_HEADS, HEAD_SIZE)
    gradient_heads = gradient_block.astype(jnp.float32).reshape(row_count_total, KEY_VALUE_HEADS, share_ratio, HEAD_SIZE)
    logit_scores = jnp.einsum('euaz,nuz->uaen', heads_queries, heads_keys) * score_scale
    position = jnp.arange(row_count_total, dtype=jnp.int32)
    allowed = (segment[:, None] == segment[None, :]) & (position[None, :] <= position[:, None])
    logit_scores = jnp.where(allowed, logit_scores, -1e+30)
    highest = lax.optimization_barrier(jnp.max(logit_scores, axis=-1, keepdims=True))
    expo = jnp.exp(logit_scores - highest)
    probs = expo / lax.optimization_barrier(jnp.sum(expo, axis=-1, keepdims=True))
    probs_reduced = lax.optimization_barrier(probs.astype(jnp.bfloat16)).astype(jnp.float32)
    attention_output = jnp.einsum('yxmd,dya->myxa', probs_reduced, heads_values).reshape(row_count_total, QUERY_HEADS * HEAD_SIZE).astype(jnp.bfloat16)
    gradient_probs = jnp.einsum('euaz,nuz->uaen', gradient_heads, heads_values)
    value_gradient = jnp.einsum('lbjm,jlbw->mlw', probs_reduced, gradient_heads).reshape(row_count_total, KEY_VALUE_HEADS * HEAD_SIZE).astype(jnp.bfloat16)
    inner = lax.optimization_barrier(jnp.sum(probs * gradient_probs, axis=-1, keepdims=True))
    gradient_scores = (probs * (gradient_probs - inner) * score_scale).astype(jnp.bfloat16)
    gradient_scores = lax.optimization_barrier(gradient_scores).astype(jnp.float32)
    query_gradient = jnp.einsum('yxmd,dya->myxa', gradient_scores, heads_keys).reshape(row_count_total, QUERY_HEADS * HEAD_SIZE).astype(jnp.bfloat16)
    key_gradient = jnp.einsum('lbjm,jlbw->mlw', gradient_scores, heads_queries).reshape(row_count_total, KEY_VALUE_HEADS * HEAD_SIZE).astype(jnp.bfloat16)
    return (attention_output, query_gradient, key_gradient, value_gradient)

def reference(rollout_rows, lengths, dest, offset, query, key_rows, value_weight, d_out):
    device_ids = jnp.arange(SHARDS, dtype=jnp.int32)
    starts = jnp.cumsum(lengths, axis=1) - lengths
    row_ids = jnp.arange(TOK_DEV, dtype=jnp.int32)
    which = (lax.optimization_barrier(jnp.sum((row_ids[None, :, None] >= starts[:, None, :]).astype(jnp.int32), axis=2)) - 1).astype(jnp.int32)
    start_of = jnp.take_along_axis(starts, which, axis=1)
    dest_of = jnp.take_along_axis(dest, which, axis=1)
    offset_of = jnp.take_along_axis(offset, which, axis=1)
    column = (device_ids % N_FSDP)[:, None]
    learner_row = ((dest_of * N_FSDP + column) * TOK_DEV + offset_of + row_ids[None, :] - start_of).astype(jnp.int32)
    flat_rows = learner_row.reshape(-1)
    learner_rows = jnp.zeros((TOKEN_ROWS, D), jnp.bfloat16).at[flat_rows].set(rollout_rows)
    sender = jnp.broadcast_to((device_ids // N_FSDP)[:, None], (SHARDS, TOK_DEV)).reshape(-1).astype(jnp.int32)
    segment = jnp.zeros((TOKEN_ROWS,), jnp.int32).at[flat_rows].set(sender)
    values = jnp.dot(learner_rows, value_weight, preferred_element_type=jnp.float32).astype(jnp.bfloat16)

    def per_device(pieces):
        return attend(*pieces)
    attention_output, query_gradient, key_gradient, value_gradient = lax.map(per_device, (query.reshape(SHARDS, TOK_DEV, QW), key_rows.reshape(SHARDS, TOK_DEV, KVW), values.reshape(SHARDS, TOK_DEV, KVW), segment.reshape(SHARDS, TOK_DEV), d_out.reshape(SHARDS, TOK_DEV, QW)))
    value_gradient = value_gradient.reshape(TOKEN_ROWS, KVW)
    grad_input = lax.dot_general(value_gradient, value_weight, (((1,), (1,)), ((), ())), preferred_element_type=jnp.float32).astype(jnp.bfloat16)
    grad_weight = lax.dot_general(learner_rows, value_gradient, (((0,), (0,)), ((), ())), preferred_element_type=jnp.float32) * (1.0 / math.sqrt(TOKEN_ROWS))
    return (attention_output.reshape(TOKEN_ROWS, QW), query_gradient.reshape(TOKEN_ROWS, QW), key_gradient.reshape(TOKEN_ROWS, KVW), grad_input, grad_weight)
```

```python
import math

import jax
import jax.numpy as jnp
from jax import lax
from jax.sharding import PartitionSpec as P

HEAD_SIZE = 128
QUERY_HEADS = 32
KEY_VALUE_HEADS = 4


def attend(block_queries, block_keys, block_values, segment, gradient_block):
    row_count_total = block_queries.shape[0]
    share_ratio = QUERY_HEADS // KEY_VALUE_HEADS
    score_scale = 1.0 / math.sqrt(HEAD_SIZE)
    heads_queries = block_queries.reshape(row_count_total, KEY_VALUE_HEADS, share_ratio, HEAD_SIZE)
    heads_keys = block_keys.reshape(row_count_total, KEY_VALUE_HEADS, HEAD_SIZE)
    heads_values = block_values.reshape(row_count_total, KEY_VALUE_HEADS, HEAD_SIZE)
    gradient_heads = gradient_block.reshape(
        row_count_total, KEY_VALUE_HEADS, share_ratio, HEAD_SIZE
    )
    logit_scores = (
        jnp.einsum("euaz,nuz->uaen", heads_queries, heads_keys, preferred_element_type=jnp.float32)
        * score_scale
    )
    position = jnp.arange(row_count_total, dtype=jnp.int32)
    allowed = (segment[:, None] == segment[None, :]) & (position[None, :] <= position[:, None])
    logit_scores = jnp.where(allowed, logit_scores, -1e30)
    highest = jnp.max(logit_scores, axis=-1, keepdims=True)
    expo = jnp.exp(logit_scores - highest)
    probs = expo / jnp.sum(expo, axis=-1, keepdims=True)
    probs_reduced = probs.astype(jnp.bfloat16)
    attention_output = jnp.einsum(
        "yxmd,dya->myxa", probs_reduced, heads_values, preferred_element_type=jnp.float32
    )
    attention_output = attention_output.reshape(row_count_total, QUERY_HEADS * HEAD_SIZE).astype(
        jnp.bfloat16
    )
    gradient_probs = jnp.einsum(
        "euaz,nuz->uaen", gradient_heads, heads_values, preferred_element_type=jnp.float32
    )
    value_gradient = jnp.einsum(
        "lbjm,jlbw->mlw", probs_reduced, gradient_heads, preferred_element_type=jnp.float32
    )
    value_gradient = value_gradient.reshape(row_count_total, KEY_VALUE_HEADS * HEAD_SIZE).astype(
        jnp.bfloat16
    )
    inner = jnp.sum(probs * gradient_probs, axis=-1, keepdims=True)
    gradient_scores = (probs * (gradient_probs - inner) * score_scale).astype(jnp.bfloat16)
    query_gradient = jnp.einsum(
        "yxmd,dya->myxa", gradient_scores, heads_keys, preferred_element_type=jnp.float32
    )
    key_gradient = jnp.einsum(
        "lbjm,jlbw->mlw", gradient_scores, heads_queries, preferred_element_type=jnp.float32
    )
    return (
        attention_output,
        query_gradient.reshape(row_count_total, QUERY_HEADS * HEAD_SIZE).astype(jnp.bfloat16),
        key_gradient.reshape(row_count_total, KEY_VALUE_HEADS * HEAD_SIZE).astype(jnp.bfloat16),
        value_gradient,
    )


def tables(plan, tok_rows):
    seq_len, dest, offset = plan[:, 0], plan[:, 1], plan[:, 2]
    order = jnp.arange(seq_len.shape[1], dtype=jnp.int32)
    earlier = order[None, :] < order[:, None]
    starts = jnp.sum(jnp.where(earlier[None], seq_len[:, None, :], 0), axis=2)
    rows = jnp.arange(tok_rows, dtype=jnp.int32)[None, :, None]
    inside = (rows >= starts[:, None, :]) & (rows < (starts + seq_len)[:, None, :])
    landing = (dest * tok_rows + offset - starts)[:, None, :] + rows
    return jnp.sum(jnp.where(inside, landing, 0), axis=2).reshape(-1)


def senders(plan, me, tok_rows):
    seq_len, dest, offset = plan[:, 0], plan[:, 1], plan[:, 2]
    mine = dest == me
    land_off = jnp.sum(jnp.where(mine, offset, 0), axis=1)
    land_len = jnp.sum(jnp.where(mine, seq_len, 0), axis=1)
    rows = jnp.arange(tok_rows, dtype=jnp.int32)[:, None]
    inside = (rows >= land_off[None, :]) & (rows < (land_off + land_len)[None, :])
    source = jnp.arange(plan.shape[0], dtype=jnp.int32)
    return jnp.sum(jnp.where(inside, source[None, :], 0), axis=1)


def local(rollout_rows, lengths, dest, offset, query, key_rows, value_weight, d_out):
    n_dp = lax.axis_size("dp")
    n_fsdp = lax.axis_size("fsdp")
    me = lax.axis_index("dp")
    tok_rows = rollout_rows.shape[0]
    column = tok_rows * n_dp
    plan = lax.all_gather(jnp.concatenate([lengths, dest, offset], axis=0), "dp", axis=0)
    shared = lax.all_to_all(rollout_rows, "dp", split_axis=1, concat_axis=0, tiled=True)
    block = value_weight.shape[0] // n_dp
    piece = lax.dynamic_slice_in_dim(value_weight, me * block, block, axis=0)
    pairs = [(a * n_fsdp + b, b * n_dp + a) for a in range(n_dp) for b in range(n_fsdp)]
    piece = lax.ppermute(piece, ("dp", "fsdp"), pairs)
    weight = lax.all_gather(piece, "fsdp", axis=0, tiled=True)
    landing = tables(plan, tok_rows)
    pick = (jnp.arange(column, dtype=jnp.int32)[:, None] == landing[None, :]).astype(jnp.bfloat16)
    rows = jnp.dot(pick, shared, preferred_element_type=jnp.float32).astype(jnp.bfloat16)
    partial = jnp.dot(rows, weight, preferred_element_type=jnp.float32).astype(jnp.bfloat16)
    parts = lax.all_to_all(
        partial.reshape(n_dp, tok_rows, partial.shape[1]), "dp", split_axis=0, concat_axis=0, tiled=True
    )
    values = jnp.sum(parts.astype(jnp.float32), axis=0).astype(jnp.bfloat16)
    attention_output, query_gradient, key_gradient, value_gradient = attend(
        query, key_rows, values, senders(plan, me, tok_rows), d_out
    )
    gathered = lax.all_gather(value_gradient, "dp", axis=0, tiled=True)
    grad_weight = lax.psum_scatter(
        lax.dot_general(
            rows, gathered, (((0,), (0,)), ((), ())), preferred_element_type=jnp.float32
        ),
        "fsdp",
        scatter_dimension=0,
        tiled=True,
    )
    grad_weight = grad_weight * (1.0 / math.sqrt(column * n_fsdp))
    share = lax.dot_general(
        gathered, weight, (((1,), (1,)), ((), ())), preferred_element_type=jnp.float32
    ).astype(jnp.bfloat16)
    grad_input = lax.all_to_all(share, "dp", split_axis=0, concat_axis=1, tiled=True)
    return (attention_output, query_gradient, key_gradient, grad_input, grad_weight)


def solution(mesh):
    in_specs = (
        P(("dp", "fsdp"), None),
        P(("dp", "fsdp"), None),
        P(("dp", "fsdp"), None),
        P(("dp", "fsdp"), None),
        P(("dp", "fsdp"), None),
        P(("dp", "fsdp"), None),
        P("fsdp", None),
        P(("dp", "fsdp"), None),
    )
    out_specs = (
        P(("dp", "fsdp"), None),
        P(("dp", "fsdp"), None),
        P(("dp", "fsdp"), None),
        P(("dp", "fsdp"), None),
        P(("dp", "fsdp"), None),
    )
    return jax.shard_map(local, mesh=mesh, in_specs=in_specs, out_specs=out_specs, check_vma=False)
```

```python
import functools
import math

import jax
import jax.numpy as jnp
from jax import lax
from jax.experimental import pallas as pl
from jax.experimental.pallas import tpu as pltpu
from jax.sharding import PartitionSpec as P

HEAD_SIZE = 128
QUERY_HEADS = 32
KEY_VALUE_HEADS = 4
MESH = pl.DeviceIdType.MESH
F32 = jnp.float32
BF16 = jnp.bfloat16


def dot(a, b, contract):
    return lax.dot_general(a, b, ((contract[:1], contract[1:]), ((), ())), preferred_element_type=F32)


def kernel(
    n_dp, n_fsdp, scale,
    x_ref, landing_ref, q_ref, k_ref, w_ref, d_ref,
    out_ref, gq_ref, gk_ref, gi_ref, gw_ref,
    shared, land, weight, pick, part, part_out, parts, values, probs, gathered, share, gwp, gwr,
    x_send, x_recv, l_send, l_recv, p_send, p_recv, g_send, g_recv, i_send, i_recv,
    w_send, w_recv, s_send, s_recv, perm_send, perm_recv, local_sem,
):
    a = lax.axis_index("dp")
    b = lax.axis_index("fsdp")
    tok = x_ref.shape[0]
    cols = shared.shape[2]
    block = cols // n_fsdp
    group = QUERY_HEADS // KEY_VALUE_HEADS
    given = b * n_dp + a
    to_a, to_b = given // n_fsdp, given % n_fsdp
    taken = a * n_fsdp + b
    from_a, from_b = taken % n_dp, taken // n_dp
    away = given != taken

    def dp_peer(i):
        return lax.rem(a + i, n_dp)

    def fsdp_peer(i):
        return lax.rem(b + i, n_fsdp)

    def over_dp(body):
        lax.fori_loop(1, n_dp, lambda i, c: (body(dp_peer(i)), c)[1], 0)

    def over_fsdp(body):
        lax.fori_loop(1, n_fsdp, lambda i, c: (body(fsdp_peer(i)), c)[1], 0)

    barrier = pltpu.get_barrier_semaphore()
    over_dp(lambda p: pl.semaphore_signal(barrier, inc=1, device_id={"dp": p}, device_id_type=MESH))
    over_fsdp(lambda p: pl.semaphore_signal(barrier, inc=1, device_id={"fsdp": p}, device_id_type=MESH))

    @pl.when(away)
    def _():
        pl.semaphore_signal(
            barrier, inc=1, device_id={"dp": from_a, "fsdp": from_b}, device_id_type=MESH
        )
        pl.semaphore_wait(barrier, n_dp + n_fsdp - 1)

    @pl.when(jnp.logical_not(away))
    def _():
        pl.semaphore_wait(barrier, n_dp + n_fsdp - 2)

    def remote(src, dst, send, recv, **where):
        return pltpu.make_async_remote_copy(
            src_ref=src, dst_ref=dst, send_sem=send, recv_sem=recv, device_id=where, device_id_type=MESH
        )

    def columns(p):
        return pl.ds(pl.multiple_of(p * cols, cols), cols)

    def x_copy(p, slot):
        return remote(x_ref.at[:, columns(p)], shared.at[slot], x_send.at[p], x_recv.at[slot], dp=p)

    def l_copy(p, slot):
        return remote(landing_ref, land.at[slot], l_send.at[p], l_recv.at[slot], dp=p)

    def p_copy(p, slot):
        return remote(part_out.at[p], parts.at[slot], p_send.at[p], p_recv.at[slot], dp=p)

    def g_copy(p, slot):
        return remote(gathered.at[a], gathered.at[slot], g_send.at[p], g_recv.at[slot], dp=p)

    def i_copy(p, slot):
        return remote(share.at[p], gi_ref.at[:, columns(slot)], i_send.at[p], i_recv.at[slot], dp=p)

    def w_copy(p, slot):
        return remote(weight.at[b], weight.at[slot], w_send.at[p], w_recv.at[slot], fsdp=p)

    def s_copy(p, slot):
        return remote(gwp.at[p], gwr.at[slot], s_send.at[p], s_recv.at[slot], fsdp=p)

    piece = w_ref.at[pl.ds(pl.multiple_of(a * block, block), block), :]
    perm = remote(piece, weight.at[to_b], perm_send, perm_recv, dp=to_a, fsdp=to_b)
    perm_in = remote(piece, weight.at[b], perm_send, perm_recv, dp=to_a, fsdp=to_b)
    perm_own = pltpu.make_async_copy(piece, weight.at[b], local_sem.at[1])

    @pl.when(away)
    def _():
        perm.start()

    @pl.when(jnp.logical_not(away))
    def _():
        perm_own.start()

    over_dp(lambda p: l_copy(p, a).start())
    over_dp(lambda p: x_copy(p, a).start())
    own = pltpu.make_async_copy(x_ref.at[:, columns(a)], shared.at[a], local_sem.at[0])
    own.start()
    land[a] = landing_ref[...]

    over_dp(lambda p: l_copy(p, p).wait_recv())
    line = lax.broadcasted_iota(jnp.int32, (n_dp * tok, tok), 0)
    for p in range(n_dp):
        hit = line == land[p][0:1, :]
        pick[:, p * tok : (p + 1) * tok] = jnp.where(hit, 1.0, 0.0).astype(BF16)

    @pl.when(away)
    def _():
        perm_in.wait_recv()

    @pl.when(jnp.logical_not(away))
    def _():
        perm_own.wait()

    over_fsdp(lambda p: w_copy(p, b).start())

    mine = pick[pl.ds(pl.multiple_of(a * tok, tok), tok), :]
    source = lax.broadcasted_iota(jnp.int32, (n_dp * tok, 128), 0) // tok
    lane = lax.broadcasted_iota(jnp.int32, (n_dp * tok, 128), 1)
    sender = dot(mine, jnp.where(source == lane, 1.0, 0.0).astype(BF16), (1, 0)).astype(BF16)
    same = dot(sender, sender, (1, 1)) > 0.5
    t_id = lax.broadcasted_iota(jnp.int32, (tok, tok), 0)
    s_id = lax.broadcasted_iota(jnp.int32, (tok, tok), 1)
    bias = jnp.where(same & (s_id <= t_id), 0.0, -1e30)
    root = 1.0 / math.sqrt(HEAD_SIZE)

    def head(g, i):
        return pl.ds(pl.multiple_of((g * group + i) * HEAD_SIZE, HEAD_SIZE), HEAD_SIZE)

    def stacked(ref, g):
        return jnp.concatenate([ref[:, head(g, i)] for i in range(group)], axis=0)

    def kv(g):
        return pl.ds(pl.multiple_of(g * HEAD_SIZE, HEAD_SIZE), HEAD_SIZE)

    def forward(g, c):
        logits = dot(stacked(q_ref, g), k_ref[:, kv(g)], (1, 1)) * root
        logits = logits.reshape(group, tok, tok)
        logits = jnp.where(bias[None] < 0.0, -1e30, logits)
        expo = jnp.exp(logits - jnp.max(logits, axis=-1, keepdims=True))
        probs[g] = (expo / jnp.sum(expo, axis=-1, keepdims=True)).reshape(group * tok, tok)
        return c

    lax.fori_loop(0, KEY_VALUE_HEADS, forward, 0)

    over_fsdp(lambda p: w_copy(p, p).wait_recv())
    full = weight[...].reshape(cols, weight.shape[2])
    own.wait()
    part[a] = dot(shared[a], full, (1, 0)).astype(BF16)

    def project(p):
        x_copy(p, p).wait_recv()
        part[p] = dot(shared[p], full, (1, 0)).astype(BF16)

    over_dp(project)
    every = part[...].reshape(n_dp * tok, part.shape[2])

    def order(p):
        return dot(pick[pl.ds(pl.multiple_of(p * tok, tok), tok), :], every, (1, 0)).astype(BF16)

    def deal(p):
        part_out[p] = order(p)
        p_copy(p, a).start()

    over_dp(deal)
    parts[a] = order(a)
    over_dp(lambda p: p_copy(p, p).wait_recv())
    total = parts[0].astype(F32)
    for p in range(1, n_dp):
        total += parts[p].astype(F32)
    values[...] = total.astype(BF16)

    def backward(g, c):
        v = values[:, kv(g)]
        d = stacked(d_ref, g)
        pr = probs[g]
        pb = pr.astype(BF16)
        att = dot(pb, v, (1, 0)).astype(BF16)
        gathered[a, :, kv(g)] = dot(pb, d, (0, 0)).astype(BF16)
        dp = dot(d, v, (1, 1))
        inner = jnp.sum(pr * dp, axis=-1, keepdims=True)
        ds = (pr * (dp - inner) * root).astype(BF16)
        gq = dot(ds, k_ref[:, kv(g)], (1, 0)).astype(BF16)
        gk_ref[:, kv(g)] = dot(ds, stacked(q_ref, g), (0, 0)).astype(BF16)
        for i in range(group):
            out_ref[:, head(g, i)] = att[i * tok : (i + 1) * tok]
            gq_ref[:, head(g, i)] = gq[i * tok : (i + 1) * tok]
        return c

    lax.fori_loop(0, KEY_VALUE_HEADS, backward, 0)

    over_dp(lambda p: g_copy(p, a).start())
    share[a] = dot(gathered[a], full, (1, 1)).astype(BF16)
    keep = pltpu.make_async_copy(share.at[a], gi_ref.at[:, columns(a)], local_sem.at[2])
    keep.start()

    def spread(p):
        g_copy(p, p).wait_recv()
        share[p] = dot(gathered[p], full, (1, 1)).astype(BF16)
        i_copy(p, a).start()

    over_dp(spread)
    learned = gathered[...].reshape(n_dp * tok, gathered.shape[2])
    back = dot(pick[...], learned, (0, 0)).astype(BF16)
    tokens = shared[...].reshape(n_dp * tok, cols)
    gwp[...] = dot(tokens, back, (0, 0)).reshape(n_fsdp, block, back.shape[1])
    over_fsdp(lambda p: s_copy(p, b).start())
    gwr[b] = gwp[b]
    over_fsdp(lambda p: s_copy(p, p).wait_recv())
    grad = gwr[0]
    for p in range(1, n_fsdp):
        grad += gwr[p]
    gw_ref[...] = grad * scale

    over_dp(lambda p: i_copy(p, p).wait_recv())
    keep.wait()

    def drain(p):
        x_copy(p, a).wait_send()
        l_copy(p, a).wait_send()
        p_copy(p, a).wait_send()
        g_copy(p, a).wait_send()
        i_copy(p, a).wait_send()

    over_dp(drain)

    def drain_fsdp(p):
        w_copy(p, b).wait_send()
        s_copy(p, b).wait_send()

    over_fsdp(drain_fsdp)

    @pl.when(away)
    def _():
        perm.wait_send()


def local(rollout_rows, lengths, dest, offset, query, key_rows, value_weight, d_out):
    n_dp = lax.axis_size("dp")
    n_fsdp = lax.axis_size("fsdp")
    tok, width = rollout_rows.shape
    kvw = value_weight.shape[1]
    cols = width // n_dp
    block = cols // n_fsdp
    seq = lengths.shape[1]
    order = jnp.arange(seq, dtype=jnp.int32)
    starts = jnp.sum(jnp.where(order[None, :] < order[:, None], lengths, 0), axis=1)[:, None]
    rows = jnp.arange(tok, dtype=jnp.int32)[None, :]
    inside = (rows >= starts) & (rows < starts + lengths[0][:, None])
    place = (dest[0] * tok + offset[0])[:, None] - starts + rows
    landing = jnp.sum(jnp.where(inside, place, 0), axis=0)
    landing = jnp.broadcast_to(landing[None, :], (8, tok))
    vmem = pl.BlockSpec(memory_space=pltpu.VMEM)
    hbm = pl.BlockSpec(memory_space=pl.ANY)
    dma = pltpu.SemaphoreType.DMA
    shape = jax.ShapeDtypeStruct
    group = QUERY_HEADS // KEY_VALUE_HEADS
    return pl.pallas_call(
        functools.partial(kernel, n_dp, n_fsdp, 1.0 / math.sqrt(tok * n_dp * n_fsdp)),
        out_shape=(
            shape(query.shape, BF16),
            shape(query.shape, BF16),
            shape(key_rows.shape, BF16),
            shape(rollout_rows.shape, BF16),
            shape((block, kvw), F32),
        ),
        in_specs=[hbm, vmem, vmem, vmem, hbm, vmem],
        out_specs=(vmem, vmem, vmem, hbm, vmem),
        scratch_shapes=[
            pltpu.VMEM((n_dp, tok, cols), BF16),
            pltpu.VMEM((n_dp, 8, tok), jnp.int32),
            pltpu.VMEM((n_fsdp, block, kvw), BF16),
            pltpu.VMEM((n_dp * tok, n_dp * tok), BF16),
            pltpu.VMEM((n_dp, tok, kvw), BF16),
            pltpu.VMEM((n_dp, tok, kvw), BF16),
            pltpu.VMEM((n_dp, tok, kvw), BF16),
            pltpu.VMEM((tok, kvw), BF16),
            pltpu.VMEM((KEY_VALUE_HEADS, group * tok, tok), F32),
            pltpu.VMEM((n_dp, tok, kvw), BF16),
            pltpu.VMEM((n_dp, tok, cols), BF16),
            pltpu.VMEM((n_fsdp, block, kvw), F32),
            pltpu.VMEM((n_fsdp, block, kvw), F32),
        ]
        + [dma((n_dp,))] * 10
        + [dma((n_fsdp,))] * 4
        + [dma, dma, dma((3,))],
        compiler_params=pltpu.CompilerParams(
            collective_id=0, has_side_effects=True, vmem_limit_bytes=56 * 1024 * 1024
        ),
    )(rollout_rows, landing, query, key_rows, value_weight, d_out)


def solution(mesh):
    rows = P(("dp", "fsdp"), None)
    return jax.shard_map(
        local,
        mesh=mesh,
        in_specs=(rows, rows, rows, rows, rows, rows, P("fsdp", None), rows),
        out_specs=(rows,) * 5,
        check_vma=False,
    )
```

```python
import functools
import math

import jax
import jax.numpy as jnp
from jax import lax
from jax.experimental import pallas as pl
from jax.experimental.pallas import tpu as pltpu
from jax.sharding import PartitionSpec as P

HEAD_SIZE = 128
QUERY_HEADS = 32
KEY_VALUE_HEADS = 4
MESH = pl.DeviceIdType.MESH
F32 = jnp.float32
BF16 = jnp.bfloat16


def dot(a, b, contract):
    return lax.dot_general(a, b, ((contract[:1], contract[1:]), ((), ())), preferred_element_type=F32)


def kernel(
    n_dp, n_fsdp, scale,
    x_ref, landing_ref, q_ref, k_ref, w_ref, d_ref,
    out_ref, gq_ref, gk_ref, gi_ref, gw_ref,
    shared, land, weight, pick, part, part_out, parts, values, probs, gathered, share, gwp, gws, gwr,
    x_send, x_recv, l_send, l_recv, p_send, p_recv, g_send, g_recv, i_send, i_recv,
    w_send, w_recv, s_send, s_recv, perm_send, perm_recv, local_sem,
):
    a = lax.axis_index("dp")
    b = lax.axis_index("fsdp")
    tok = x_ref.shape[0]
    cols = shared.shape[2]
    block = cols // n_fsdp
    group = QUERY_HEADS // KEY_VALUE_HEADS
    given = b * n_dp + a
    to_a, to_b = given // n_fsdp, given % n_fsdp
    taken = a * n_fsdp + b
    from_a, from_b = taken % n_dp, taken // n_dp
    away = given != taken

    def dp_peer(i):
        return lax.rem(a + i, n_dp)

    def fsdp_peer(i):
        return lax.rem(b + i, n_fsdp)

    def over_dp(body):
        lax.fori_loop(1, n_dp, lambda i, c: (body(dp_peer(i)), c)[1], 0)

    def over_fsdp(body):
        lax.fori_loop(1, n_fsdp, lambda i, c: (body(fsdp_peer(i)), c)[1], 0)

    barrier = pltpu.get_barrier_semaphore()
    over_dp(lambda p: pl.semaphore_signal(barrier, inc=1, device_id={"dp": p}, device_id_type=MESH))
    over_fsdp(lambda p: pl.semaphore_signal(barrier, inc=1, device_id={"fsdp": p}, device_id_type=MESH))

    @pl.when(away)
    def _():
        pl.semaphore_signal(
            barrier, inc=1, device_id={"dp": from_a, "fsdp": from_b}, device_id_type=MESH
        )
        pl.semaphore_wait(barrier, n_dp + n_fsdp - 1)

    @pl.when(jnp.logical_not(away))
    def _():
        pl.semaphore_wait(barrier, n_dp + n_fsdp - 2)

    def remote(src, dst, send, recv, **where):
        return pltpu.make_async_remote_copy(
            src_ref=src, dst_ref=dst, send_sem=send, recv_sem=recv, device_id=where, device_id_type=MESH
        )

    def columns(p):
        return pl.ds(pl.multiple_of(p * cols, cols), cols)

    def x_copy(p, slot):
        return remote(x_ref.at[:, columns(p)], shared.at[slot], x_send.at[p], x_recv.at[slot], dp=p)

    def l_copy(p, slot):
        return remote(landing_ref, land.at[slot], l_send.at[p], l_recv.at[slot], dp=p)

    def p_copy(p, slot):
        return remote(part_out.at[p], parts.at[slot], p_send.at[p], p_recv.at[slot], dp=p)

    def g_copy(p, slot):
        return remote(gathered.at[a], gathered.at[slot], g_send.at[p], g_recv.at[slot], dp=p)

    def i_copy(p, slot):
        return remote(share.at[p], gi_ref.at[:, columns(slot)], i_send.at[p], i_recv.at[slot], dp=p)

    def w_copy(p, slot, sem):
        return remote(weight.at[slot], weight.at[slot], w_send.at[sem], w_recv.at[slot], fsdp=p)

    has_left, has_right = b > 0, b < n_fsdp - 1

    def s_copy(p, slot):
        return remote(gws.at[p], gwr.at[slot], s_send.at[p], s_recv.at[slot], fsdp=p)

    piece = w_ref.at[pl.ds(pl.multiple_of(a * block, block), block), :]
    perm = remote(piece, weight.at[to_b], perm_send, perm_recv, dp=to_a, fsdp=to_b)
    perm_in = remote(piece, weight.at[b], perm_send, perm_recv, dp=to_a, fsdp=to_b)
    perm_own = pltpu.make_async_copy(piece, weight.at[b], local_sem.at[1])

    @pl.when(away)
    def _():
        perm.start()

    @pl.when(jnp.logical_not(away))
    def _():
        perm_own.start()

    over_dp(lambda p: l_copy(p, a).start())
    over_dp(lambda p: x_copy(p, a).start())
    own = pltpu.make_async_copy(x_ref.at[:, columns(a)], shared.at[a], local_sem.at[0])
    own.start()
    land[a] = landing_ref[...]

    over_dp(lambda p: l_copy(p, p).wait_recv())
    line = lax.broadcasted_iota(jnp.int32, (n_dp * tok, tok), 0)
    for p in range(n_dp):
        hit = line == land[p][0:1, :]
        pick[:, p * tok : (p + 1) * tok] = jnp.where(hit, 1.0, 0.0).astype(BF16)

    mine = pick[pl.ds(pl.multiple_of(a * tok, tok), tok), :]
    source = lax.broadcasted_iota(jnp.int32, (n_dp * tok, 128), 0) // tok
    lane = lax.broadcasted_iota(jnp.int32, (n_dp * tok, 128), 1)
    sender = dot(mine, jnp.where(source == lane, 1.0, 0.0).astype(BF16), (1, 0)).astype(BF16)
    same = dot(sender, sender, (1, 1)) > 0.5
    t_id = lax.broadcasted_iota(jnp.int32, (tok, tok), 0)
    s_id = lax.broadcasted_iota(jnp.int32, (tok, tok), 1)
    bias = jnp.where(same & (s_id <= t_id), 0.0, -1e30)
    root = 1.0 / math.sqrt(HEAD_SIZE)

    def head(g, i):
        return pl.ds(pl.multiple_of((g * group + i) * HEAD_SIZE, HEAD_SIZE), HEAD_SIZE)

    def stacked(ref, g):
        return jnp.concatenate([ref[:, head(g, i)] for i in range(group)], axis=0)

    def kv(g):
        return pl.ds(pl.multiple_of(g * HEAD_SIZE, HEAD_SIZE), HEAD_SIZE)

    def forward(g, c):
        logits = dot(stacked(q_ref, g), k_ref[:, kv(g)], (1, 1)) * root
        logits = logits.reshape(group, tok, tok)
        logits = jnp.where(bias[None] < 0.0, -1e30, logits)
        expo = jnp.exp(logits - jnp.max(logits, axis=-1, keepdims=True))
        probs[g] = (expo / jnp.sum(expo, axis=-1, keepdims=True)).reshape(group * tok, tok)
        return c

    lax.fori_loop(0, KEY_VALUE_HEADS, forward, 0)

    @pl.when(away)
    def _():
        perm_in.wait_recv()

    @pl.when(jnp.logical_not(away))
    def _():
        perm_own.wait()

    @pl.when(has_right)
    def _():
        w_copy(b + 1, b, b).start()

    @pl.when(has_left)
    def _():
        w_copy(b - 1, b, n_fsdp).start()

    for step in range(1, n_fsdp):

        @pl.when(b >= step)
        def _():
            w_copy(b - 1, b - step, b - step).wait_recv()

            @pl.when(has_right)
            def _():
                w_copy(b + 1, b - step, b - step).start()

        @pl.when(b + step < n_fsdp)
        def _():
            w_copy(b + 1, b + step, b + step).wait_recv()

            @pl.when(has_left)
            def _():
                w_copy(b - 1, b + step, b + step).start()

    full = weight[...].reshape(cols, weight.shape[2])
    own.wait()
    part[a] = dot(shared[a], full, (1, 0)).astype(BF16)

    def project(p):
        x_copy(p, p).wait_recv()
        part[p] = dot(shared[p], full, (1, 0)).astype(BF16)

    over_dp(project)
    every = part[...].reshape(n_dp * tok, part.shape[2])

    def order(p):
        return dot(pick[pl.ds(pl.multiple_of(p * tok, tok), tok), :], every, (1, 0)).astype(BF16)

    def deal(p):
        part_out[p] = order(p)
        p_copy(p, a).start()

    over_dp(deal)
    parts[a] = order(a)
    over_dp(lambda p: p_copy(p, p).wait_recv())
    total = parts[0].astype(F32)
    for p in range(1, n_dp):
        total += parts[p].astype(F32)
    values[...] = total.astype(BF16)

    def backward(g, c):
        v = values[:, kv(g)]
        d = stacked(d_ref, g)
        pr = probs[g]
        pb = pr.astype(BF16)
        att = dot(pb, v, (1, 0)).astype(BF16)
        gathered[a, :, kv(g)] = dot(pb, d, (0, 0)).astype(BF16)
        dp = dot(d, v, (1, 1))
        inner = jnp.sum(pr * dp, axis=-1, keepdims=True)
        ds = (pr * (dp - inner) * root).astype(BF16)
        gq = dot(ds, k_ref[:, kv(g)], (1, 0)).astype(BF16)
        gk_ref[:, kv(g)] = dot(ds, stacked(q_ref, g), (0, 0)).astype(BF16)
        for i in range(group):
            out_ref[:, head(g, i)] = att[i * tok : (i + 1) * tok]
            gq_ref[:, head(g, i)] = gq[i * tok : (i + 1) * tok]
        return c

    lax.fori_loop(0, KEY_VALUE_HEADS, backward, 0)

    over_dp(lambda p: g_copy(p, a).start())
    share[a] = dot(gathered[a], full, (1, 1)).astype(BF16)
    keep = pltpu.make_async_copy(share.at[a], gi_ref.at[:, columns(a)], local_sem.at[2])
    keep.start()

    def spread(p):
        g_copy(p, p).wait_recv()
        share[p] = dot(gathered[p], full, (1, 1)).astype(BF16)
        i_copy(p, a).start()

    over_dp(spread)
    learned = gathered[...].reshape(n_dp * tok, gathered.shape[2])
    back = dot(pick[...], learned, (0, 0)).astype(BF16)
    tokens = shared[...].reshape(n_dp * tok, cols)
    gwp[...] = dot(tokens, back, (0, 0)).reshape(n_fsdp, block, back.shape[1])
    gws[...] = gwp[...].astype(BF16)
    over_fsdp(lambda p: s_copy(p, b).start())
    gwr[b] = jnp.zeros_like(gwr[b])
    over_fsdp(lambda p: s_copy(p, p).wait_recv())
    grad = gwp[b]
    for p in range(n_fsdp):
        grad += gwr[p].astype(F32)
    gw_ref[...] = grad * scale

    over_dp(lambda p: i_copy(p, p).wait_recv())
    keep.wait()

    def drain(p):
        x_copy(p, a).wait_send()
        l_copy(p, a).wait_send()
        p_copy(p, a).wait_send()
        g_copy(p, a).wait_send()
        i_copy(p, a).wait_send()

    over_dp(drain)

    def drain_fsdp(p):
        s_copy(p, b).wait_send()

    over_fsdp(drain_fsdp)

    @pl.when(has_right)
    def _():
        w_copy(b + 1, b, b).wait_send()

    @pl.when(has_left)
    def _():
        w_copy(b - 1, b, n_fsdp).wait_send()

    for step in range(1, n_fsdp):

        @pl.when((b >= step) & has_right)
        def _():
            w_copy(b + 1, b - step, b - step).wait_send()

        @pl.when((b + step < n_fsdp) & has_left)
        def _():
            w_copy(b - 1, b + step, b + step).wait_send()

    @pl.when(away)
    def _():
        perm.wait_send()


def local(rollout_rows, lengths, dest, offset, query, key_rows, value_weight, d_out):
    n_dp = lax.axis_size("dp")
    n_fsdp = lax.axis_size("fsdp")
    tok, width = rollout_rows.shape
    kvw = value_weight.shape[1]
    cols = width // n_dp
    block = cols // n_fsdp
    seq = lengths.shape[1]
    order = jnp.arange(seq, dtype=jnp.int32)
    starts = jnp.sum(jnp.where(order[None, :] < order[:, None], lengths, 0), axis=1)[:, None]
    rows = jnp.arange(tok, dtype=jnp.int32)[None, :]
    inside = (rows >= starts) & (rows < starts + lengths[0][:, None])
    place = (dest[0] * tok + offset[0])[:, None] - starts + rows
    landing = jnp.sum(jnp.where(inside, place, 0), axis=0)
    landing = jnp.broadcast_to(landing[None, :], (8, tok))
    vmem = pl.BlockSpec(memory_space=pltpu.VMEM)
    hbm = pl.BlockSpec(memory_space=pl.ANY)
    dma = pltpu.SemaphoreType.DMA
    shape = jax.ShapeDtypeStruct
    group = QUERY_HEADS // KEY_VALUE_HEADS
    return pl.pallas_call(
        functools.partial(kernel, n_dp, n_fsdp, 1.0 / math.sqrt(tok * n_dp * n_fsdp)),
        out_shape=(
            shape(query.shape, BF16),
            shape(query.shape, BF16),
            shape(key_rows.shape, BF16),
            shape(rollout_rows.shape, BF16),
            shape((block, kvw), F32),
        ),
        in_specs=[hbm, vmem, vmem, vmem, hbm, vmem],
        out_specs=(vmem, vmem, vmem, hbm, vmem),
        scratch_shapes=[
            pltpu.VMEM((n_dp, tok, cols), BF16),
            pltpu.VMEM((n_dp, 8, tok), jnp.int32),
            pltpu.VMEM((n_fsdp, block, kvw), BF16),
            pltpu.VMEM((n_dp * tok, n_dp * tok), BF16),
            pltpu.VMEM((n_dp, tok, kvw), BF16),
            pltpu.VMEM((n_dp, tok, kvw), BF16),
            pltpu.VMEM((n_dp, tok, kvw), BF16),
            pltpu.VMEM((tok, kvw), BF16),
            pltpu.VMEM((KEY_VALUE_HEADS, group * tok, tok), F32),
            pltpu.VMEM((n_dp, tok, kvw), BF16),
            pltpu.VMEM((n_dp, tok, cols), BF16),
            pltpu.VMEM((n_fsdp, block, kvw), F32),
            pltpu.VMEM((n_fsdp, block, kvw), BF16),
            pltpu.VMEM((n_fsdp, block, kvw), BF16),
        ]
        + [dma((n_dp,))] * 10
        + [dma((n_fsdp + 1,))]
        + [dma((n_fsdp,))] * 3
        + [dma, dma, dma((3,))],
        compiler_params=pltpu.CompilerParams(
            collective_id=0, has_side_effects=True, vmem_limit_bytes=56 * 1024 * 1024
        ),
    )(rollout_rows, landing, query, key_rows, value_weight, d_out)


def solution(mesh):
    rows = P(("dp", "fsdp"), None)
    return jax.shard_map(
        local,
        mesh=mesh,
        in_specs=(rows, rows, rows, rows, rows, rows, P("fsdp", None), rows),
        out_specs=(rows,) * 5,
        check_vma=False,
    )
```

```python
import functools
import math

import jax
import jax.numpy as jnp
from jax import lax
from jax.experimental import pallas as pl
from jax.experimental.pallas import tpu as pltpu
from jax.sharding import PartitionSpec as P

HEAD_SIZE = 128
PIECES = 2
QUERY_HEADS = 32
KEY_VALUE_HEADS = 4
MESH = pl.DeviceIdType.MESH
F32 = jnp.float32
BF16 = jnp.bfloat16


def dot(a, b, contract):
    return lax.dot_general(a, b, ((contract[:1], contract[1:]), ((), ())), preferred_element_type=F32)


def kernel(
    n_dp, n_fsdp, scale,
    x_ref, landing_ref, q_ref, k_ref, w_ref, d_ref,
    out_ref, gq_ref, gk_ref, gi_ref, gw_ref,
    shared, land, weight, pick, part, part_out, parts, values, probs, gathered, share, gwp, gws, gwr,
    x_send, x_recv, l_send, l_recv, p_send, p_recv, g_send, g_recv, i_send, i_recv,
    w_send, w_recv, s_send, s_recv, perm_send, perm_recv, perm_local, local_sem,
):
    a = lax.axis_index("dp")
    b = lax.axis_index("fsdp")
    tok = x_ref.shape[0]
    cols = shared.shape[2]
    block = cols // n_fsdp
    group = QUERY_HEADS // KEY_VALUE_HEADS
    given = b * n_dp + a
    to_a, to_b = given // n_fsdp, given % n_fsdp
    taken = a * n_fsdp + b
    from_a, from_b = taken % n_dp, taken // n_dp
    away = given != taken

    def dp_peer(i):
        return lax.rem(a + i, n_dp)

    def fsdp_peer(i):
        return lax.rem(b + i, n_fsdp)

    def over_dp(body):
        lax.fori_loop(1, n_dp, lambda i, c: (body(dp_peer(i)), c)[1], 0)

    def over_fsdp(body):
        lax.fori_loop(1, n_fsdp, lambda i, c: (body(fsdp_peer(i)), c)[1], 0)

    barrier = pltpu.get_barrier_semaphore()
    over_dp(lambda p: pl.semaphore_signal(barrier, inc=1, device_id={"dp": p}, device_id_type=MESH))
    over_fsdp(lambda p: pl.semaphore_signal(barrier, inc=1, device_id={"fsdp": p}, device_id_type=MESH))

    @pl.when(away)
    def _():
        pl.semaphore_signal(
            barrier, inc=1, device_id={"dp": from_a, "fsdp": from_b}, device_id_type=MESH
        )
        pl.semaphore_wait(barrier, n_dp + n_fsdp - 1)

    @pl.when(jnp.logical_not(away))
    def _():
        pl.semaphore_wait(barrier, n_dp + n_fsdp - 2)

    def remote(src, dst, send, recv, **where):
        return pltpu.make_async_remote_copy(
            src_ref=src, dst_ref=dst, send_sem=send, recv_sem=recv, device_id=where, device_id_type=MESH
        )

    def columns(p):
        return pl.ds(pl.multiple_of(p * cols, cols), cols)

    def x_copy(p, slot):
        return remote(x_ref.at[:, columns(p)], shared.at[slot], x_send.at[p], x_recv.at[slot], dp=p)

    def l_copy(p, slot):
        return remote(landing_ref, land.at[slot], l_send.at[p], l_recv.at[slot], dp=p)

    def p_copy(p, slot):
        return remote(part_out.at[p], parts.at[slot], p_send.at[p], p_recv.at[slot], dp=p)

    def g_copy(p, slot):
        return remote(gathered.at[a], gathered.at[slot], g_send.at[p], g_recv.at[slot], dp=p)

    def i_copy(p, slot):
        return remote(share.at[p], gi_ref.at[:, columns(slot)], i_send.at[p], i_recv.at[slot], dp=p)

    def w_copy(p, slot, sem, c):
        rows = weight.at[slot, pl.ds(c * part_rows, part_rows)]
        return remote(rows, rows, w_send.at[c, sem], w_recv.at[c, slot], fsdp=p)

    has_left, has_right = b > 0, b < n_fsdp - 1

    def s_copy(p, slot):
        return remote(gws.at[p], gwr.at[slot], s_send.at[p], s_recv.at[slot], fsdp=p)

    part_rows = block // PIECES

    def piece(c):
        return w_ref.at[pl.ds(pl.multiple_of(a * block + c * part_rows, part_rows), part_rows), :]

    def perm(c, slot):
        rows = weight.at[slot, pl.ds(c * part_rows, part_rows)]
        return remote(piece(c), rows, perm_send.at[c], perm_recv.at[c], dp=to_a, fsdp=to_b)

    def perm_own(c):
        return pltpu.make_async_copy(
            piece(c), weight.at[b, pl.ds(c * part_rows, part_rows)], perm_local.at[c]
        )

    @pl.when(away)
    def _():
        for c in range(PIECES):
            perm(c, to_b).start()

    @pl.when(jnp.logical_not(away))
    def _():
        for c in range(PIECES):
            perm_own(c).start()

    over_dp(lambda p: l_copy(p, a).start())
    over_dp(lambda p: x_copy(p, a).start())
    own = pltpu.make_async_copy(x_ref.at[:, columns(a)], shared.at[a], local_sem.at[0])
    own.start()
    land[a] = landing_ref[...]

    over_dp(lambda p: l_copy(p, p).wait_recv())
    line = lax.broadcasted_iota(jnp.int32, (n_dp * tok, tok), 0)
    for p in range(n_dp):
        hit = line == land[p][0:1, :]
        pick[:, p * tok : (p + 1) * tok] = jnp.where(hit, 1.0, 0.0).astype(BF16)

    mine = pick[pl.ds(pl.multiple_of(a * tok, tok), tok), :]
    source = lax.broadcasted_iota(jnp.int32, (n_dp * tok, 128), 0) // tok
    lane = lax.broadcasted_iota(jnp.int32, (n_dp * tok, 128), 1)
    sender = dot(mine, jnp.where(source == lane, 1.0, 0.0).astype(BF16), (1, 0)).astype(BF16)
    same = dot(sender, sender, (1, 1)) > 0.5
    t_id = lax.broadcasted_iota(jnp.int32, (tok, tok), 0)
    s_id = lax.broadcasted_iota(jnp.int32, (tok, tok), 1)
    bias = jnp.where(same & (s_id <= t_id), 0.0, -1e30)
    root = 1.0 / math.sqrt(HEAD_SIZE)

    def head(g, i):
        return pl.ds(pl.multiple_of((g * group + i) * HEAD_SIZE, HEAD_SIZE), HEAD_SIZE)

    def stacked(ref, g):
        return jnp.concatenate([ref[:, head(g, i)] for i in range(group)], axis=0)

    def kv(g):
        return pl.ds(pl.multiple_of(g * HEAD_SIZE, HEAD_SIZE), HEAD_SIZE)

    def forward(g, c):
        logits = dot(stacked(q_ref, g), k_ref[:, kv(g)], (1, 1)) * root
        logits = logits.reshape(group, tok, tok)
        logits = jnp.where(bias[None] < 0.0, -1e30, logits)
        expo = jnp.exp(logits - jnp.max(logits, axis=-1, keepdims=True))
        probs[g] = (expo / jnp.sum(expo, axis=-1, keepdims=True)).reshape(group * tok, tok)
        return c

    lax.fori_loop(0, KEY_VALUE_HEADS, forward, 0)

    for c in range(PIECES):

        @pl.when(away)
        def _(c=c):
            perm(c, b).wait_recv()

        @pl.when(jnp.logical_not(away))
        def _(c=c):
            perm_own(c).wait()

        @pl.when(has_right)
        def _(c=c):
            w_copy(b + 1, b, b, c).start()

        @pl.when(has_left)
        def _(c=c):
            w_copy(b - 1, b, n_fsdp, c).start()

    for step in range(1, n_fsdp):
        for c in range(PIECES):

            @pl.when(b >= step)
            def _(c=c, step=step):
                w_copy(b - 1, b - step, b - step, c).wait_recv()

                @pl.when(has_right)
                def _():
                    w_copy(b + 1, b - step, b - step, c).start()

            @pl.when(b + step < n_fsdp)
            def _(c=c, step=step):
                w_copy(b + 1, b + step, b + step, c).wait_recv()

                @pl.when(has_left)
                def _():
                    w_copy(b - 1, b + step, b + step, c).start()

    full = weight[...].reshape(cols, weight.shape[2])
    own.wait()
    part[a] = dot(shared[a], full, (1, 0)).astype(BF16)

    def project(p):
        x_copy(p, p).wait_recv()
        part[p] = dot(shared[p], full, (1, 0)).astype(BF16)

    over_dp(project)
    every = part[...].reshape(n_dp * tok, part.shape[2])

    def order(p):
        return dot(pick[pl.ds(pl.multiple_of(p * tok, tok), tok), :], every, (1, 0)).astype(BF16)

    def deal(p):
        part_out[p] = order(p)
        p_copy(p, a).start()

    over_dp(deal)
    parts[a] = order(a)
    over_dp(lambda p: p_copy(p, p).wait_recv())
    total = parts[0].astype(F32)
    for p in range(1, n_dp):
        total += parts[p].astype(F32)
    values[...] = total.astype(BF16)

    def backward(g, c):
        v = values[:, kv(g)]
        d = stacked(d_ref, g)
        pr = probs[g]
        pb = pr.astype(BF16)
        att = dot(pb, v, (1, 0)).astype(BF16)
        gathered[a, :, kv(g)] = dot(pb, d, (0, 0)).astype(BF16)
        dp = dot(d, v, (1, 1))
        inner = jnp.sum(pr * dp, axis=-1, keepdims=True)
        ds = (pr * (dp - inner) * root).astype(BF16)
        gq = dot(ds, k_ref[:, kv(g)], (1, 0)).astype(BF16)
        gk_ref[:, kv(g)] = dot(ds, stacked(q_ref, g), (0, 0)).astype(BF16)
        for i in range(group):
            out_ref[:, head(g, i)] = att[i * tok : (i + 1) * tok]
            gq_ref[:, head(g, i)] = gq[i * tok : (i + 1) * tok]
        return c

    lax.fori_loop(0, KEY_VALUE_HEADS, backward, 0)

    over_dp(lambda p: g_copy(p, a).start())
    share[a] = dot(gathered[a], full, (1, 1)).astype(BF16)
    keep = pltpu.make_async_copy(share.at[a], gi_ref.at[:, columns(a)], local_sem.at[2])
    keep.start()

    def spread(p):
        g_copy(p, p).wait_recv()
        share[p] = dot(gathered[p], full, (1, 1)).astype(BF16)
        i_copy(p, a).start()

    over_dp(spread)
    learned = gathered[...].reshape(n_dp * tok, gathered.shape[2])
    back = dot(pick[...], learned, (0, 0)).astype(BF16)
    tokens = shared[...].reshape(n_dp * tok, cols)
    gwp[...] = dot(tokens, back, (0, 0)).reshape(n_fsdp, block, back.shape[1])
    gws[...] = gwp[...].astype(BF16)
    over_fsdp(lambda p: s_copy(p, b).start())
    gwr[b] = jnp.zeros_like(gwr[b])
    over_fsdp(lambda p: s_copy(p, p).wait_recv())
    grad = gwp[b]
    for p in range(n_fsdp):
        grad += gwr[p].astype(F32)
    gw_ref[...] = grad * scale

    over_dp(lambda p: i_copy(p, p).wait_recv())
    keep.wait()

    def drain(p):
        x_copy(p, a).wait_send()
        l_copy(p, a).wait_send()
        p_copy(p, a).wait_send()
        g_copy(p, a).wait_send()
        i_copy(p, a).wait_send()

    over_dp(drain)

    def drain_fsdp(p):
        s_copy(p, b).wait_send()

    over_fsdp(drain_fsdp)

    for c in range(PIECES):

        @pl.when(away)
        def _(c=c):
            perm(c, to_b).wait_send()

        @pl.when(has_right)
        def _(c=c):
            w_copy(b + 1, b, b, c).wait_send()

        @pl.when(has_left)
        def _(c=c):
            w_copy(b - 1, b, n_fsdp, c).wait_send()

        for step in range(1, n_fsdp):

            @pl.when((b >= step) & has_right)
            def _(c=c, step=step):
                w_copy(b + 1, b - step, b - step, c).wait_send()

            @pl.when((b + step < n_fsdp) & has_left)
            def _(c=c, step=step):
                w_copy(b - 1, b + step, b + step, c).wait_send()


def local(rollout_rows, lengths, dest, offset, query, key_rows, value_weight, d_out):
    n_dp = lax.axis_size("dp")
    n_fsdp = lax.axis_size("fsdp")
    tok, width = rollout_rows.shape
    kvw = value_weight.shape[1]
    cols = width // n_dp
    block = cols // n_fsdp
    seq = lengths.shape[1]
    order = jnp.arange(seq, dtype=jnp.int32)
    starts = jnp.sum(jnp.where(order[None, :] < order[:, None], lengths, 0), axis=1)[:, None]
    rows = jnp.arange(tok, dtype=jnp.int32)[None, :]
    inside = (rows >= starts) & (rows < starts + lengths[0][:, None])
    place = (dest[0] * tok + offset[0])[:, None] - starts + rows
    landing = jnp.sum(jnp.where(inside, place, 0), axis=0)
    landing = jnp.broadcast_to(landing[None, :], (8, tok))
    vmem = pl.BlockSpec(memory_space=pltpu.VMEM)
    hbm = pl.BlockSpec(memory_space=pl.ANY)
    dma = pltpu.SemaphoreType.DMA
    shape = jax.ShapeDtypeStruct
    group = QUERY_HEADS // KEY_VALUE_HEADS
    return pl.pallas_call(
        functools.partial(kernel, n_dp, n_fsdp, 1.0 / math.sqrt(tok * n_dp * n_fsdp)),
        out_shape=(
            shape(query.shape, BF16),
            shape(query.shape, BF16),
            shape(key_rows.shape, BF16),
            shape(rollout_rows.shape, BF16),
            shape((block, kvw), F32),
        ),
        in_specs=[hbm, vmem, vmem, vmem, hbm, vmem],
        out_specs=(vmem, vmem, vmem, hbm, vmem),
        scratch_shapes=[
            pltpu.VMEM((n_dp, tok, cols), BF16),
            pltpu.VMEM((n_dp, 8, tok), jnp.int32),
            pltpu.VMEM((n_fsdp, block, kvw), BF16),
            pltpu.VMEM((n_dp * tok, n_dp * tok), BF16),
            pltpu.VMEM((n_dp, tok, kvw), BF16),
            pltpu.VMEM((n_dp, tok, kvw), BF16),
            pltpu.VMEM((n_dp, tok, kvw), BF16),
            pltpu.VMEM((tok, kvw), BF16),
            pltpu.VMEM((KEY_VALUE_HEADS, group * tok, tok), F32),
            pltpu.VMEM((n_dp, tok, kvw), BF16),
            pltpu.VMEM((n_dp, tok, cols), BF16),
            pltpu.VMEM((n_fsdp, block, kvw), F32),
            pltpu.VMEM((n_fsdp, block, kvw), BF16),
            pltpu.VMEM((n_fsdp, block, kvw), BF16),
        ]
        + [dma((n_dp,))] * 10
        + [dma((PIECES, n_fsdp + 1)), dma((PIECES, n_fsdp))]
        + [dma((n_fsdp,))] * 2
        + [dma((PIECES,))] * 3
        + [dma((3,))],
        compiler_params=pltpu.CompilerParams(
            collective_id=0, has_side_effects=True, vmem_limit_bytes=56 * 1024 * 1024
        ),
    )(rollout_rows, landing, query, key_rows, value_weight, d_out)


def solution(mesh):
    rows = P(("dp", "fsdp"), None)
    return jax.shard_map(
        local,
        mesh=mesh,
        in_specs=(rows, rows, rows, rows, rows, rows, P("fsdp", None), rows),
        out_specs=(rows,) * 5,
        check_vma=False,
    )
```
